512 devices in a mesh: rep: 32 (over y, z_hi, core), exp: 16 (over z_lo, x).
Axes of the slice: x: 4, y: 4, z: 16 (z_hi: 4, z_lo: 4; z = z_hi * 4 + z_lo), core: 2. Of those that a mesh axis runs over, the one named last changes fastest.
Arguments:
- tokens: bfloat16 [32, 2048, 1024], P('rep', 'exp'), may hold values from -6 to 6
- cotangent: bfloat16 [32, 2048, 1024], P('rep', 'exp'), may hold values from -4 to 4
- route_ids: int32 [32, 2048, 2], P('rep', 'exp'), may hold values from 0 to 3, all different within a row; in each aligned block of 128 rows (0 to 127, 128 to 255, ..., all dimensions but the last counted through in order) at most 96 rows name the same one
- route_weights: bfloat16 [32, 2048, 2], P('rep', 'exp'), may hold values from 0.19921875 to 1
- gate_weight: bfloat16 [32, 1024, 5632], P('rep', None, 'exp'), may hold values from -0.1875 to 0.1875
- up_weight: bfloat16 [32, 1024, 5632], P('rep', None, 'exp'), may hold values from -0.1875 to 0.1875
- down_weight: bfloat16 [32, 5632, 1024], P('rep', 'exp'), may hold values from -0.15625 to 0.15625
- tracker: bfloat16 [32, 5632, 1024], P('rep', 'exp'), may hold values from -12 to 12
- grad_prev: bfloat16 [32, 5632, 1024], P('rep', 'exp'), may hold values from -12 to 12
- gossip_step: int32 [3], replicated, may hold values from 0 to 2
Outputs:
- token_grad: bfloat16 [32, 2048, 1024], P('rep', 'exp')
- tracker_new: bfloat16 [32, 5632, 1024], P('rep', 'exp')
The draws below stay inside these ranges and needn't reach their ends.
Inputs may be any that keep to these rules, and one draw needn't show every extreme that they name: `route_ids`: each token names 2 different experts; within each aligned block of 128 tokens of a replica no expert is named by more than 96 tokens, and in some block one expert is named by exactly 96.
All inputs are finite; a program needn't handle non-finite values.
Results may differ from the reference program's by a relative error of at most 0.0058.
Values may be sent and summed in bfloat16 or wider, within the bound.
A program may use at most 64 MiB of HBM per device.

```python
import math
import jax
import jax.numpy as jnp
import numpy as np
from jax import lax

D = 1024
HID = 1408
EXPERTS = 4
TOP = 2
ROUNDS = 3
TOK_DEV = 128
CAP = 96
GROUP = 4
HID_DEV = 352
TOKENS = 2048
N_REP = 32
N_EXP = 16


def levels(key, shape, cuts, least, top_value):
    loudness, own = 1.0, jax.random.fold_in(key, 6)
    for dim, parts in cuts:
        draws = jnp.exp(jax.random.uniform(jax.random.fold_in(own, dim), (parts,), jnp.float32, least / len(cuts), top_value / len(cuts)))
        loudness = loudness * jnp.repeat(draws, shape[dim] // parts).reshape([-1 if axis == dim else 1 for axis in range(len(shape))])
    return loudness


def assign_block(key, own, number, rows, count, top, reach, lean):
    ranking = jax.random.permutation(key, count)
    crowded, ordinary = shares(count, rows * top, reach, lean, True), shares(count, rows * top, reach, lean, False)
    places = jnp.arange(count)

    def named(lengths, rotation):
        used = int((lengths > 0).sum())
        fixed = max(1, used // 4)
        shifted = fixed + (places - fixed + rotation * (used - fixed)) % max(1, count - fixed)
        return jnp.zeros((count,), jnp.int32).at[ranking[jnp.where(places < fixed, places, shifted)]].set(jnp.asarray(lengths, jnp.int32))

    lengths = jnp.where(number % 4 == 0, named(crowded, number // 4), named(ordinary, number - number // 4 - 1))
    mixed = jax.random.permutation(jax.random.fold_in(own, 3), count)
    source_of, receiver = mixed[0:count // 2 * 2:2], mixed[1:count // 2 * 2:2]
    room = jnp.minimum(lengths[source_of] - 1, reach - lengths[receiver]) // 2
    room = jnp.where((source_of == ranking[0]) | (receiver == ranking[0]) | (lengths[receiver] == 0), 0, jnp.maximum(room, 0))
    shifted = jax.random.randint(jax.random.fold_in(own, 4), (count // 2,), 0, 1 << 20) % (room + 1)
    lengths = lengths.at[source_of].add(-shifted).at[receiver].add(shifted)
    labels = jnp.searchsorted(jnp.cumsum(lengths), jnp.arange(rows * top), side="right").astype(jnp.int32)
    table = labels.reshape(top, rows).T
    table = table[jax.random.permutation(jax.random.fold_in(own, 1), rows)]
    rotation = jax.random.randint(jax.random.fold_in(own, 2), (rows, 1), 0, top)
    return jnp.take_along_axis(table, (jnp.arange(top)[None, :] + rotation) % top, axis=1)


def shares(amount, total, reach, slope, full):
    loads = [(1 << 20) // math.isqrt(standing ** slope) + 1 for standing in range(1, amount + 1)]
    largest = reach if full else min(reach, max(-(-total // amount), total * loads[0] // sum(loads)))
    least = 1 if total - largest >= amount - 1 else 0
    given, spare = [largest] + [least] * (amount - 1), total - largest - least * (amount - 1)
    while spare > 0:
        candidates = [i for i in range(1, amount) if given[i] < largest] or [i for i in range(1, amount) if given[i] < reach]
        pool, budget = sum([loads[i] for i in candidates]), spare
        for i in candidates:
            addition = min(reach - given[i], max(1, budget * loads[i] // pool), spare)
            given[i] = given[i] + addition
            spare = spare - addition
    return np.array(given)


def gaussian(key, shape, deviation, most, pieces=(), held_as=jnp.bfloat16):
    drawn = jax.random.normal(key, shape, jnp.float32) * deviation
    if len(pieces) > 0:
        drawn = levels(key, shape, pieces, -0.22, 0.18) * drawn
    return jnp.clip(drawn, min=-most, max=most).astype(held_as)


def setup_inputs(seed: int = 0) -> dict:
    keys = jax.random.split(jax.random.key(seed), 11)
    tokens = gaussian(keys[0], (N_REP, TOKENS, D), 1.0, 6.0, ((0, 32), (1, 16)))
    cotangent = gaussian(keys[1], (N_REP, TOKENS, D), 0.5, 4.0, ((0, 32), (1, 16)))
    route_ids_keys = jax.random.split(jax.random.fold_in(keys[2], 1), N_REP * TOKENS // TOK_DEV)
    route_ids_turns = jax.random.permutation(jax.random.fold_in(keys[2], 3), N_REP * TOKENS // TOK_DEV)
    route_ids = jax.vmap(lambda own, number: assign_block(jax.random.fold_in(keys[2], 2), own, number, TOK_DEV, EXPERTS, TOP, CAP, 2))(route_ids_keys, route_ids_turns).reshape((N_REP, TOKENS, TOP))
    route_weights = jnp.clip(0.19921875 + 0.80078125 * jax.random.uniform(keys[3], (N_REP, TOKENS, TOP), jnp.float32) ** levels(keys[3], (N_REP, TOKENS, TOP), ((0, 32), (1, 16)), -0.2, 0.2), 0.19921875, 1.0).astype(jnp.bfloat16)
    gate_weight = gaussian(keys[4], (N_REP, D, EXPERTS * HID), D ** -0.5, 0.1875, ((0, 32), (2, 16)))
    up_weight = gaussian(keys[5], (N_REP, D, EXPERTS * HID), D ** -0.5, 0.1875, ((0, 32), (2, 16)))
    down_weight = gaussian(keys[6], (N_REP, EXPERTS * HID, D), HID ** -0.5, 0.15625, ((0, 32), (1, 16)))
    tracker = gaussian(keys[7], (N_REP, EXPERTS * HID, D), 2.0, 12.0, ((0, 32), (1, 16)))
    grad_prev = gaussian(keys[8], (N_REP, EXPERTS * HID, D), 2.0, 12.0, ((0, 32), (1, 16)))
    gossip_step = jax.random.randint(keys[9], (ROUNDS,), 0, 3).astype(jnp.int32)
    return {"tokens": tokens, "cotangent": cotangent, "route_ids": route_ids, "route_weights": route_weights, "gate_weight": gate_weight, "up_weight": up_weight, "down_weight": down_weight, "tracker": tracker, "grad_prev": grad_prev, "gossip_step": gossip_step}


def slot_table(block_ids):
    hits = (block_ids[:, :, None] == jnp.arange(EXPERTS, dtype=jnp.int32)).astype(jnp.int32)
    flat_hits = hits.reshape(-1, EXPERTS)
    ranked = jnp.cumsum(flat_hits, axis=0) - 1
    within = jnp.sum(flat_hits * ranked, axis=-1).reshape(block_ids.shape)
    return (block_ids * CAP + within).astype(jnp.int32)


def fill_rows(values, slots):
    width = values.shape[-1]
    rows = jnp.broadcast_to(values[:, None, :], (TOK_DEV, TOP, width)).reshape(-1, width)
    return jnp.zeros((EXPERTS * CAP, width), values.dtype).at[slots.reshape(-1)].set(rows)


def fill_coef(weights, slots):
    return jnp.zeros((EXPERTS * CAP,), weights.dtype).at[slots.reshape(-1)].set(weights.reshape(-1))


def by_expert(buffer):
    width = buffer.shape[-1]
    return buffer.reshape(N_EXP, EXPERTS, CAP, width).transpose(1, 0, 2, 3).reshape(EXPERTS, N_EXP * CAP, width)


def one_replica(inputs):
    tokens, cotangent, route_ids, route_weights, gate_weight, up_weight, down_weight = inputs
    slots = jax.vmap(slot_table)(route_ids.reshape(N_EXP, TOK_DEV, TOP))
    in_rows = by_expert(jax.vmap(fill_rows)(tokens.reshape(N_EXP, TOK_DEV, D), slots))
    cot_rows = by_expert(jax.vmap(fill_rows)(cotangent.reshape(N_EXP, TOK_DEV, D), slots))
    coef_rows = jax.vmap(fill_coef)(route_weights.reshape(N_EXP, TOK_DEV, TOP), slots)
    coef_rows = coef_rows.reshape(N_EXP, EXPERTS, CAP).transpose(1, 0, 2).reshape(EXPERTS, N_EXP * CAP)
    grads = []
    combined = []
    for expert in range(EXPERTS):
        lo = expert * HID
        w_gate = gate_weight[:, lo:lo + HID]
        w_up = up_weight[:, lo:lo + HID]
        w_down = down_weight[lo:lo + HID, :]
        x_rows = in_rows[expert]
        c_rows = cot_rows[expert]
        coef = coef_rows[expert].astype(jnp.float32)[:, None]
        gate_act = jnp.dot(x_rows, w_gate, preferred_element_type=jnp.float32)
        up_act = jnp.dot(x_rows, w_up, preferred_element_type=jnp.float32)
        sigmoid_g = jax.nn.sigmoid(gate_act)
        act = gate_act * sigmoid_g
        weighted = (coef * act * up_act).astype(jnp.bfloat16)
        grads.append(jnp.dot(weighted.T, c_rows, preferred_element_type=jnp.float32))
        hidden_grad = coef * jnp.dot(c_rows, w_down.T, preferred_element_type=jnp.float32)
        gate_grad = (hidden_grad * up_act * sigmoid_g * (1.0 + gate_act * (1.0 - sigmoid_g))).astype(jnp.bfloat16)
        up_grad = (hidden_grad * act).astype(jnp.bfloat16)
        total = jnp.zeros((N_EXP * CAP, D), jnp.float32)
        for piece in range(GROUP):
            start = piece * HID_DEV
            stop = start + HID_DEV
            partial_value = jnp.dot(gate_grad[:, start:stop], w_gate[:, start:stop].T, preferred_element_type=jnp.float32)
            partial_value = partial_value + jnp.dot(up_grad[:, start:stop], w_up[:, start:stop].T, preferred_element_type=jnp.float32)
            total = total + partial_value.astype(jnp.bfloat16).astype(jnp.float32)
        combined.append(total.reshape(N_EXP, CAP, D))
    combined = jnp.stack(combined, axis=0).transpose(1, 0, 2, 3).reshape(N_EXP, EXPERTS * CAP, D)

    def collect(rows, block_slots):
        return jnp.sum(rows[block_slots.reshape(-1)].reshape(TOK_DEV, TOP, D), axis=1)

    token_grad = jax.vmap(collect)(combined, slots).reshape(TOKENS, D).astype(jnp.bfloat16)
    return token_grad, jnp.concatenate(grads, axis=0)


def reference(tokens, cotangent, route_ids, route_weights, gate_weight, up_weight, down_weight, tracker, grad_prev, gossip_step):
    token_grad, grad = lax.map(one_replica, (tokens, cotangent, route_ids, route_weights, gate_weight, up_weight, down_weight))
    delta_share = (grad - grad_prev.astype(jnp.float32)) / ROUNDS
    mixed = tracker.astype(jnp.float32)
    replica_ids = jnp.arange(N_REP, dtype=jnp.int32)
    for round_index in range(ROUNDS):
        partner = jnp.bitwise_xor(replica_ids, jnp.left_shift(jnp.int32(1), gossip_step[round_index].astype(jnp.int32)))
        mixed = (mixed + mixed[partner]) * 0.5 + delta_share
    tracker_new = mixed.astype(jnp.bfloat16)
    return token_grad, tracker_new
```

```python
from functools import partial

import jax
import jax.numpy as jnp
from jax import lax
from jax.experimental import pallas as pl
from jax.experimental.pallas import tpu as pltpu
from jax.sharding import PartitionSpec as P

D = 1024
EXPERTS = 4
ROUNDS = 3
TOK = 128
CAP = 96
HID = 352
COLS = 4 * CAP
ORDER = (1, 3, 2)
F32 = jnp.float32
BF16 = jnp.bfloat16
NT = (((1,), (1,)), ((), ()))
TN = (((0,), (0,)), ((), ()))
NN = (((1,), (0,)), ((), ()))


def dot(a, b, dims=NN):
    return lax.dot_general(a, b, dims, preferred_element_type=F32)


def layer_kernel(
    tok_ref,
    cot_ref,
    ids_ref,
    wts_ref,
    gate_ref,
    up_ref,
    down_ref,
    out_ref,
    grad_ref,
    stage,
    spread,
    rows,
    weights,
    gu,
    hd,
    gug,
    wtd,
    part,
    grads,
    gsend,
    grecv,
    psend,
    precv,
    ret,
    zsend,
    z_ss,
    z_rs,
    a_ss,
    a_rs,
    w_ss,
    w_rs,
    g_ss,
    g_rs,
    p_ss,
    p_rs,
    r_ss,
    r_rs,
):
    rep = lax.axis_index("rep")
    e = lax.axis_index("exp")
    z = e // 4
    x = e - 4 * z
    odd = x % 2
    pair = e + 1 - 2 * odd
    mate = 4 * z + (x + 3 + 2 * odd) % 4

    def at_z(d):
        return 4 * ((z + d) % 4) + x

    def send(src, dst, ss, rs, to):
        return pltpu.make_async_remote_copy(
            src_ref=src,
            dst_ref=dst,
            send_sem=ss,
            recv_sem=rs,
            device_id=(rep, to),
            device_id_type=pl.DeviceIdType.MESH,
        )

    barrier = pltpu.get_barrier_semaphore()
    for peer in (at_z(1), at_z(2), at_z(3), pair, mate):
        pl.semaphore_signal(
            barrier, inc=1, device_id=(rep, peer), device_id_type=pl.DeviceIdType.MESH
        )

    weights[0, 0:HID] = gate_ref[...].T
    pl.semaphore_wait(barrier, 5)

    def w_copy(i):
        piece = pl.ds(i * HID, HID)
        return send(weights.at[0, piece], weights.at[1, piece], w_ss.at[i], w_rs.at[i], mate)

    w_copy(0).start()

    lane = lax.broadcasted_iota(jnp.int32, (TOK, TOK), 1)
    sub = lax.broadcasted_iota(jnp.int32, (TOK, TOK), 0)
    id0 = ids_ref[:, 0:1]
    id1 = ids_ref[:, 1:2]
    hit0 = (lane == id0).astype(F32)
    hit1 = (lane == id1).astype(F32)
    wts = wts_ref[...].astype(F32)
    hits = (hit0 + hit1).astype(BF16)
    coefs = (hit0 * wts[:, 0:1] + hit1 * wts[:, 1:2]).astype(BF16)
    eye = (sub == lane).astype(F32).astype(BF16)
    before = (sub < lane).astype(F32).astype(BF16)
    hit_t = dot(hits, eye, TN)[0:8]
    rank_t = dot(hits, before, TN)[0:8]
    coef_t = dot(coefs, eye, TN)[0:8]
    expert = lax.broadcasted_iota(jnp.int32, (8, TOK), 0)
    slot = lax.broadcasted_iota(jnp.int32, (CAP, TOK), 0).astype(F32)

    def place(d):
        mine = expert == (z + d) % 4
        zero = jnp.zeros((8, TOK), F32)
        hit = jnp.sum(jnp.where(mine, hit_t, zero), axis=0, keepdims=True)
        rank = jnp.sum(jnp.where(mine, rank_t, zero), axis=0, keepdims=True)
        coef = jnp.sum(jnp.where(mine, coef_t, zero), axis=0, keepdims=True)
        placed = jnp.where(slot == rank, 1.0, 0.0) * hit
        plain = placed.astype(BF16)
        spread[d * CAP:(d + 1) * CAP] = plain
        t = dot(plain, tok_ref[...]).astype(BF16)
        c = dot((placed * coef).astype(BF16), cot_ref[...]).astype(BF16)
        return t, c

    def z_copy(d):
        return send(stage.at[d], rows.at[0, :, z], z_ss.at[d], z_rs.at[d], at_z(d))

    def z_arrive(d):
        return send(stage.at[d], rows.at[0, :, (z + 4 - d) % 4], z_ss.at[d], z_rs.at[d], at_z(d))

    def a_copy(d):
        zs = (z + 4 - d) % 4
        return send(rows.at[0, :, zs], rows.at[1, :, zs], a_ss.at[d], a_rs.at[d], pair)

    for d in (2, 1, 3):
        t, c = place(d)
        stage[d, 0] = t
        stage[d, 1] = c
        z_copy(d).start()
    t, c = place(0)
    rows[0, 0, z] = t
    rows[0, 1, z] = c
    a_copy(0).start()

    weights[0, HID:2 * HID] = up_ref[...].T
    w_copy(1).start()
    weights[0, 2 * HID:3 * HID] = down_ref[...]

    for d in ORDER:
        if d == 2:
            w_copy(0).wait_send()
            w_copy(1).wait_send()
            w_copy(2).start()
        z_arrive(d).wait_recv()
        a_copy(d).start()

    def first(rg, hs):
        tk = rows[rg, 0].reshape(COLS, D)
        unit = 2 * rg + hs
        gu[unit] = dot(weights[hs, 0:2 * HID], tk, NT)

        def body(i, carry):
            at = pl.ds(pl.multiple_of(i * 32, 32), 32)
            low = pl.ds(pl.multiple_of(i * 32 + HID, 32), 32)
            g = gu[unit, at]
            u = gu[unit, low]
            wtd[at] = (g * jax.nn.sigmoid(g) * u).astype(BF16)
            return carry

        lax.fori_loop(0, HID // 32, body, 0)
        return dot(wtd[...], rows[rg, 1].reshape(COLS, D))

    def second(rg, hs):
        unit = 2 * rg + hs
        hd[...] = dot(weights[hs, 2 * HID:3 * HID], rows[rg, 1].reshape(COLS, D), NT)

        def body(i, carry):
            at = pl.ds(pl.multiple_of(i * 32, 32), 32)
            low = pl.ds(pl.multiple_of(i * 32 + HID, 32), 32)
            g = gu[unit, at]
            u = gu[unit, low]
            h = hd[at]
            s = jax.nn.sigmoid(g)
            gug[at] = (h * u * s * (1.0 + g * (1.0 - s))).astype(BF16)
            gug[low] = (h * (g * s)).astype(BF16)
            return carry

        lax.fori_loop(0, HID // 32, body, 0)
        return dot(gug[...], weights[hs, 0:2 * HID], TN)

    grads[...] = first(0, 0)
    part[0] = second(0, 0).reshape(4, CAP, D)

    w_copy(0).wait_recv()
    w_copy(1).wait_recv()
    other = first(0, 1)
    for d in range(4):
        a_copy(d).wait_recv()
    gsend[...] = (other + first(1, 1)).astype(BF16)
    g_copy = send(gsend, grecv, g_ss, g_rs, mate)
    g_copy.start()
    grads[...] += first(1, 0)

    w_copy(2).wait_recv()
    part[1] = second(1, 0).reshape(4, CAP, D)
    psend[...] = (part[1] + second(1, 1).reshape(4, CAP, D)).astype(BF16)

    def p_copy(d):
        zs = (z + d) % 4
        return send(psend.at[zs], precv.at[zs], p_ss.at[d], p_rs.at[d], pair)

    for d in (2, 1, 3, 0):
        p_copy(d).start()
    part[0] += second(0, 1).reshape(4, CAP, D)

    def r_copy(d):
        return send(zsend.at[d], ret.at[4 - d], r_ss.at[d], r_rs.at[4 - d], at_z(d))

    for d in (2, 1, 3, 0):
        p_copy(d).wait_recv()
        zs = (z + d) % 4
        total = (part[0, zs] + precv[zs].astype(F32)).astype(BF16)
        if d == 0:
            ret[0] = total
        else:
            zsend[d] = total
            r_copy(d).start()

    g_copy.wait_recv()
    grad_ref[...] = grads[...] + grecv[...].astype(F32)

    for d in (1, 3, 2):
        r_copy(d).wait_recv()
    out_ref[...] = dot(spread[...], ret[...].reshape(COLS, D), TN).astype(BF16)

    for d in (1, 2, 3):
        z_copy(d).wait_send()
        r_copy(d).wait_send()
    for d in range(4):
        a_copy(d).wait_send()
        p_copy(d).wait_send()
    w_copy(2).wait_send()
    g_copy.wait_send()


def layer(tokens, cotangent, route_ids, route_weights, gate, up, down):
    vmem = pl.BlockSpec(memory_space=pltpu.VMEM)
    dma = pltpu.SemaphoreType.DMA
    return pl.pallas_call(
        layer_kernel,
        out_shape=(
            jax.ShapeDtypeStruct((TOK, D), BF16),
            jax.ShapeDtypeStruct((HID, D), F32),
        ),
        in_specs=[vmem] * 7,
        out_specs=(vmem, vmem),
        scratch_shapes=[
            pltpu.VMEM((4, 2, CAP, D), BF16),
            pltpu.VMEM((COLS, TOK), BF16),
            pltpu.VMEM((2, 2, 4, CAP, D), BF16),
            pltpu.VMEM((2, 3 * HID, D), BF16),
            pltpu.VMEM((4, 2 * HID, COLS), F32),
            pltpu.VMEM((HID, COLS), F32),
            pltpu.VMEM((2 * HID, COLS), BF16),
            pltpu.VMEM((HID, COLS), BF16),
            pltpu.VMEM((2, 4, CAP, D), F32),
            pltpu.VMEM((HID, D), F32),
            pltpu.VMEM((HID, D), BF16),
            pltpu.VMEM((HID, D), BF16),
            pltpu.VMEM((4, CAP, D), BF16),
            pltpu.VMEM((4, CAP, D), BF16),
            pltpu.VMEM((4, CAP, D), BF16),
            pltpu.VMEM((4, CAP, D), BF16),
            dma((4,)),
            dma((4,)),
            dma((4,)),
            dma((4,)),
            dma((3,)),
            dma((3,)),
            dma,
            dma,
            dma((4,)),
            dma((4,)),
            dma((4,)),
            dma((4,)),
        ],
        compiler_params=pltpu.CompilerParams(
            collective_id=0, has_side_effects=True, vmem_limit_bytes=56 * 2**20
        ),
        cost_estimate=pl.CostEstimate(
            flops=7 * 10**9, bytes_accessed=6 * 10**6, transcendentals=10**6
        ),
    )(tokens, cotangent, route_ids, route_weights, gate, up, down)


def average(state, bit):
    count = lax.axis_size("rep")
    pairs = [(source, source ^ (1 << bit)) for source in range(count)]
    peer = lax.ppermute(state.astype(BF16), "rep", pairs)
    return (state + peer.astype(F32)) * 0.5


def shards(
    tokens,
    cotangent,
    route_ids,
    route_weights,
    gate_weight,
    up_weight,
    down_weight,
    tracker,
    grad_prev,
    gossip_step,
):
    out, grad = layer(
        tokens[0],
        cotangent[0],
        route_ids[0],
        route_weights[0],
        gate_weight[0],
        up_weight[0],
        down_weight[0],
    )
    steps = jnp.clip(gossip_step, 0, 2)
    s1, s2, s3 = steps[0], steps[1], steps[2]
    averages = [partial(average, bit=bit) for bit in range(3)]
    maybe = [lambda state: state] + averages
    mixed = tracker[0].astype(F32)
    mixed = lax.switch(jnp.where((s1 == s2) | (s1 == s3), 0, s1 + 1), maybe, mixed)
    share = (grad - grad_prev[0].astype(F32)) / ROUNDS
    mixed = lax.switch(jnp.where(s2 == s3, 0, s2 + 1), maybe, mixed + share)
    mixed = lax.switch(s3, averages, mixed + share) + share
    return (out[None], mixed.astype(BF16)[None])


def solution(mesh):
    rows = P("rep", "exp", None)
    cols = P("rep", None, "exp")
    in_specs = (rows, rows, rows, rows, cols, cols, rows, rows, rows, P())
    return jax.shard_map(
        shards, mesh=mesh, in_specs=in_specs, out_specs=(rows, rows), check_vma=False
    )
```

```python
from functools import partial

import jax
import jax.numpy as jnp
from jax import lax
from jax.experimental import pallas as pl
from jax.experimental.pallas import tpu as pltpu
from jax.sharding import PartitionSpec as P

D = 1024
EXPERTS = 4
ROUNDS = 3
TOK = 128
CAP = 96
HID = 352
COLS = 4 * CAP
ORDER = (1, 3, 2)
CHUNKS = ((0, 96), (96, 96), (192, 80), (272, 80))
LATE = ((0,), (1,), (2,), (0, 1), (0, 2), (1, 0), (1, 2), (2, 0), (2, 1))
F32 = jnp.float32
BF16 = jnp.bfloat16
NT = (((1,), (1,)), ((), ()))
TN = (((0,), (0,)), ((), ()))
NN = (((1,), (0,)), ((), ()))


def dot(a, b, dims=NN):
    return lax.dot_general(a, b, dims, preferred_element_type=F32)


def layer_kernel(
    late,
    tok_ref,
    cot_ref,
    ids_ref,
    wts_ref,
    gate_ref,
    up_ref,
    down_ref,
    tracker_ref,
    peer_ref,
    prev_ref,
    out_ref,
    new_ref,
    stage,
    spread,
    rows,
    weights,
    gu,
    hd,
    gug,
    wtd,
    part,
    grads,
    state,
    gsend,
    grecv,
    psend,
    precv,
    ret,
    zsend,
    msend,
    mrecv,
    kept,
    z_ss,
    z_rs,
    a_ss,
    a_rs,
    w_ss,
    w_rs,
    g_ss,
    g_rs,
    p_ss,
    p_rs,
    r_ss,
    r_rs,
    m_ss,
    m_rs,
    own_sem,
    kept_sem,
):
    rep = lax.axis_index("rep")
    e = lax.axis_index("exp")
    z = e // 4
    x = e - 4 * z
    odd = x % 2
    pair = e + 1 - 2 * odd
    mate = 4 * z + (x + 3 + 2 * odd) % 4

    def at_z(d):
        return 4 * ((z + d) % 4) + x

    def across(bit):
        step = 2**bit
        return rep + step * (1 - 2 * ((rep // step) % 2))

    def send(src, dst, ss, rs, to, replica=None):
        return pltpu.make_async_remote_copy(
            src_ref=src,
            dst_ref=dst,
            send_sem=ss,
            recv_sem=rs,
            device_id=(rep if replica is None else replica, to),
            device_id_type=pl.DeviceIdType.MESH,
        )

    own = [
        pltpu.make_async_copy(ref, weights.at[0, pl.ds(i * HID, HID)], own_sem.at[i])
        for i, ref in enumerate((gate_ref, up_ref, down_ref))
    ]
    keep = [
        pltpu.make_async_copy(ref, kept.at[i], kept_sem.at[i])
        for i, ref in enumerate((tracker_ref, peer_ref, prev_ref))
    ]
    barrier = pltpu.get_barrier_semaphore()
    peers = [(rep, at_z(1)), (rep, at_z(2)), (rep, at_z(3)), (rep, pair), (rep, mate)]
    peers += [(across(bit), e) for bit in late]
    for to in peers:
        pl.semaphore_signal(
            barrier, inc=1, device_id=to, device_id_type=pl.DeviceIdType.MESH
        )
    for copy in own:
        copy.start()

    lane = lax.broadcasted_iota(jnp.int32, (TOK, TOK), 1)
    sub = lax.broadcasted_iota(jnp.int32, (TOK, TOK), 0)
    before = (sub < lane).astype(F32).astype(BF16)
    expert = lax.broadcasted_iota(jnp.int32, (8, TOK), 0)
    slot = lax.broadcasted_iota(jnp.int32, (CAP, TOK), 0).astype(F32)
    ids = ids_ref[...]
    wts = wts_ref[...].astype(F32)
    hit0 = (expert == ids[0:1]).astype(F32)
    hit1 = (expert == ids[1:2]).astype(F32)
    hit_t = hit0 + hit1
    coef_t = hit0 * wts[0:1] + hit1 * wts[1:2]
    rank_t = dot(hit_t.astype(BF16), before)

    def place(d):
        mine = expert == (z + d) % 4
        zero = jnp.zeros((8, TOK), F32)
        hit = jnp.sum(jnp.where(mine, hit_t, zero), axis=0, keepdims=True)
        rank = jnp.sum(jnp.where(mine, rank_t, zero), axis=0, keepdims=True)
        coef = jnp.sum(jnp.where(mine, coef_t, zero), axis=0, keepdims=True)
        placed = jnp.where(slot == rank, 1.0, 0.0) * hit
        plain = placed.astype(BF16)
        spread[d * CAP:(d + 1) * CAP] = plain
        t = dot(plain, tok_ref[...]).astype(BF16)
        c = dot((placed * coef).astype(BF16), cot_ref[...]).astype(BF16)
        return t, c

    def w_copy(i):
        piece = pl.ds(i * HID, HID)
        return send(weights.at[0, piece], weights.at[1, piece], w_ss.at[i], w_rs.at[i], mate)

    def z_copy(d):
        return send(stage.at[d], rows.at[0, :, z], z_ss.at[d], z_rs.at[d], at_z(d))

    def z_arrive(d):
        return send(stage.at[d], rows.at[0, :, (z + 4 - d) % 4], z_ss.at[d], z_rs.at[d], at_z(d))

    def a_copy(d):
        zs = (z + 4 - d) % 4
        return send(rows.at[0, :, zs], rows.at[1, :, zs], a_ss.at[d], a_rs.at[d], pair)

    pl.semaphore_wait(barrier, len(peers))
    for i in range(2):
        own[i].wait()
        w_copy(i).start()
    for d in (1, 3, 0, 2):
        t, c = place(d)
        if d == 0:
            rows[0, 0, z] = t
            rows[0, 1, z] = c
            a_copy(0).start()
        else:
            stage[d, 0] = t
            stage[d, 1] = c
            if d != 2:
                z_copy(d).start()
    own[2].wait()
    for copy in keep:
        copy.start()

    z_copy(1).wait_send()
    z_copy(3).wait_send()
    z_copy(2).start()
    for d in ORDER:
        if d == 2:
            w_copy(0).wait_send()
            w_copy(1).wait_send()
            w_copy(2).start()
        z_arrive(d).wait_recv()
        a_copy(d).start()

    def first(rg, hs):
        tk = rows[rg, 0].reshape(COLS, D)
        unit = 2 * rg + hs
        gu[unit] = dot(weights[hs, 0:2 * HID], tk, NT)

        def body(i, carry):
            at = pl.ds(pl.multiple_of(i * 32, 32), 32)
            low = pl.ds(pl.multiple_of(i * 32 + HID, 32), 32)
            g = gu[unit, at]
            u = gu[unit, low]
            wtd[at] = (g * jax.nn.sigmoid(g) * u).astype(BF16)
            return carry

        lax.fori_loop(0, HID // 32, body, 0)
        return dot(wtd[...], rows[rg, 1].reshape(COLS, D))

    def second(rg, hs):
        unit = 2 * rg + hs
        hd[...] = dot(weights[hs, 2 * HID:3 * HID], rows[rg, 1].reshape(COLS, D), NT)

        def body(i, carry):
            at = pl.ds(pl.multiple_of(i * 32, 32), 32)
            low = pl.ds(pl.multiple_of(i * 32 + HID, 32), 32)
            g = gu[unit, at]
            u = gu[unit, low]
            h = hd[at]
            s = jax.nn.sigmoid(g)
            gug[at] = (h * u * s * (1.0 + g * (1.0 - s))).astype(BF16)
            gug[low] = (h * (g * s)).astype(BF16)
            return carry

        lax.fori_loop(0, HID // 32, body, 0)
        return dot(gug[...], weights[hs, 0:2 * HID], TN)

    grads[...] = first(0, 0)
    part[0] = second(0, 0).reshape(4, CAP, D)

    w_copy(0).wait_recv()
    w_copy(1).wait_recv()
    state[...] = first(0, 1)
    for d in range(4):
        a_copy(d).wait_recv()
    gsend[...] = (state[...] + first(1, 1)).astype(BF16)

    def chunk(c):
        return pl.ds(CHUNKS[c][0], CHUNKS[c][1])

    def g_copy(c):
        at = chunk(c)
        return send(gsend.at[at], grecv.at[at], g_ss.at[c], g_rs.at[c], mate)

    def m_copy(i, c):
        at = chunk(c)
        return send(
            msend.at[i, at], mrecv.at[i, at], m_ss.at[i, c], m_rs.at[i, c], e, across(late[i])
        )

    g_copy(0).start()
    g_copy(1).start()
    grads[...] += first(1, 0)
    for copy in keep:
        copy.wait()

    for c in range(len(CHUNKS)):
        at = chunk(c)
        if c + 2 < len(CHUNKS):
            g_copy(c).wait_send()
            g_copy(c + 2).start()
        g_copy(c).wait_recv()
        share = (grads[at] + grecv[at].astype(F32) - kept[2, at].astype(F32)) / ROUNDS
        mixed = (kept[0, at].astype(F32) + kept[1, at].astype(F32)) * 0.5
        mixed = mixed + (share if len(late) == 2 else 2.0 * share)
        grads[at] = share
        state[at] = mixed
        msend[0, at] = mixed.astype(BF16)
        m_copy(0, c).start()

    def mix(i, c):
        at = chunk(c)
        m_copy(i, c).wait_recv()
        return (state[at] + mrecv[i, at].astype(F32)) * 0.5 + grads[at]

    def pass_on():
        for c in range(len(CHUNKS)):
            at = chunk(c)
            mixed = mix(0, c)
            state[at] = mixed
            msend[1, at] = mixed.astype(BF16)
            m_copy(1, c).start()

    if len(late) == 2 and late[0] == 0:
        pass_on()

    w_copy(2).wait_recv()
    part[1] = second(1, 0).reshape(4, CAP, D)
    psend[...] = (part[1] + second(1, 1).reshape(4, CAP, D)).astype(BF16)

    def p_copy(d):
        zs = (z + d) % 4
        return send(psend.at[zs], precv.at[zs], p_ss.at[d], p_rs.at[d], pair)

    p_copy(2).start()
    p_copy(1).start()
    part[0] += second(0, 1).reshape(4, CAP, D)
    p_copy(2).wait_send()
    p_copy(3).start()
    p_copy(1).wait_send()
    p_copy(0).start()

    def r_copy(d):
        return send(zsend.at[d], ret.at[4 - d], r_ss.at[d], r_rs.at[4 - d], at_z(d))

    for d in (2, 1, 3, 0):
        p_copy(d).wait_recv()
        zs = (z + d) % 4
        total = (part[0, zs] + precv[zs].astype(F32)).astype(BF16)
        if d == 0:
            ret[0] = total
        else:
            zsend[d] = total
            r_copy(d).start()

    if len(late) == 2 and late[0] != 0:
        pass_on()
    for d in (1, 3, 2):
        r_copy(d).wait_recv()
    out_ref[...] = dot(spread[...], ret[...].reshape(COLS, D), TN).astype(BF16)
    for c in range(len(CHUNKS)):
        new_ref[chunk(c)] = mix(len(late) - 1, c).astype(BF16)

    z_copy(2).wait_send()
    p_copy(3).wait_send()
    p_copy(0).wait_send()
    for d in (1, 2, 3):
        r_copy(d).wait_send()
    for d in range(4):
        a_copy(d).wait_send()
    w_copy(2).wait_send()
    for c in range(len(CHUNKS)):
        if c >= len(CHUNKS) - 2:
            g_copy(c).wait_send()
        for i in range(len(late)):
            m_copy(i, c).wait_send()


def layer(late, number, *arrays):
    vmem = pl.BlockSpec(memory_space=pltpu.VMEM)
    hbm = pl.BlockSpec(memory_space=pl.ANY)
    dma = pltpu.SemaphoreType.DMA
    return pl.pallas_call(
        partial(layer_kernel, late),
        out_shape=(
            jax.ShapeDtypeStruct((TOK, D), BF16),
            jax.ShapeDtypeStruct((HID, D), BF16),
        ),
        in_specs=[vmem] * 4 + [hbm] * 6,
        out_specs=(vmem, vmem),
        scratch_shapes=[
            pltpu.VMEM((4, 2, CAP, D), BF16),
            pltpu.VMEM((COLS, TOK), BF16),
            pltpu.VMEM((2, 2, 4, CAP, D), BF16),
            pltpu.VMEM((2, 3 * HID, D), BF16),
            pltpu.VMEM((4, 2 * HID, COLS), F32),
            pltpu.VMEM((HID, COLS), F32),
            pltpu.VMEM((2 * HID, COLS), BF16),
            pltpu.VMEM((HID, COLS), BF16),
            pltpu.VMEM((2, 4, CAP, D), F32),
            pltpu.VMEM((HID, D), F32),
            pltpu.VMEM((HID, D), F32),
            pltpu.VMEM((HID, D), BF16),
            pltpu.VMEM((HID, D), BF16),
            pltpu.VMEM((4, CAP, D), BF16),
            pltpu.VMEM((4, CAP, D), BF16),
            pltpu.VMEM((4, CAP, D), BF16),
            pltpu.VMEM((4, CAP, D), BF16),
            pltpu.VMEM((len(late), HID, D), BF16),
            pltpu.VMEM((len(late), HID, D), BF16),
            pltpu.VMEM((3, HID, D), BF16),
            dma((4,)),
            dma((4,)),
            dma((4,)),
            dma((4,)),
            dma((3,)),
            dma((3,)),
            dma((len(CHUNKS),)),
            dma((len(CHUNKS),)),
            dma((4,)),
            dma((4,)),
            dma((4,)),
            dma((4,)),
            dma((len(late), len(CHUNKS))),
            dma((len(late), len(CHUNKS))),
            dma((3,)),
            dma((3,)),
        ],
        compiler_params=pltpu.CompilerParams(
            collective_id=number, has_side_effects=True, vmem_limit_bytes=56 * 2**20
        ),
        cost_estimate=pl.CostEstimate(
            flops=7 * 10**9, bytes_accessed=6 * 10**6, transcendentals=10**6
        ),
    )(*arrays)


def from_peer(state, bit):
    count = lax.axis_size("rep")
    pairs = [(source, source ^ (1 << bit)) for source in range(count)]
    return lax.ppermute(state, "rep", pairs)


def shards(
    tokens,
    cotangent,
    route_ids,
    route_weights,
    gate_weight,
    up_weight,
    down_weight,
    tracker,
    grad_prev,
    gossip_step,
):
    steps = jnp.clip(gossip_step, 0, 2)
    s1, s2, s3 = steps[0], steps[1], steps[2]
    maybe = [lambda state: state] + [partial(from_peer, bit=bit) for bit in range(3)]
    peer = lax.switch(jnp.where((s1 == s2) | (s1 == s3), 0, s1 + 1), maybe, tracker[0])
    pick = jnp.where(s2 == s3, s2, 3 + 2 * s2 + jnp.where(s3 > s2, s3 - 1, s3))
    out, new = lax.switch(
        pick,
        [partial(layer, late, number) for number, late in enumerate(LATE)],
        tokens[0],
        cotangent[0],
        route_ids[0].T,
        route_weights[0].T,
        gate_weight[0].T,
        up_weight[0].T,
        down_weight[0],
        tracker[0],
        peer,
        grad_prev[0],
    )
    return (out[None], new[None])


def solution(mesh):
    rows = P("rep", "exp", None)
    cols = P("rep", None, "exp")
    in_specs = (rows, rows, rows, rows, cols, cols, rows, rows, rows, P())
    return jax.shard_map(
        shards, mesh=mesh, in_specs=in_specs, out_specs=(rows, rows), check_vma=False
    )
```

```python
from functools import partial

import jax
import jax.numpy as jnp
from jax import lax
from jax.experimental import pallas as pl
from jax.experimental.pallas import tpu as pltpu
from jax.sharding import PartitionSpec as P

D = 1024
EXPERTS = 4
ROUNDS = 3
TOK = 128
CAP = 96
WIDE = 256
HID = 352
COLS = 4 * CAP
ORDER = (1, 3, 2)
CHUNKS = ((0, 96), (96, 96), (192, 80), (272, 80))
LATE = ((0,), (1,), (2,), (0, 1), (0, 2), (1, 0), (1, 2), (2, 0), (2, 1))
ALL = [(a, b, c) for a in range(3) for b in range(3) for c in range(3)]
CHOICES = (
    [0 if a in (b, c) else a + 1 for a, b, c in ALL],
    [LATE.index((b,) if b == c else (b, c)) for a, b, c in ALL],
)
F32 = jnp.float32
BF16 = jnp.bfloat16
NT = (((1,), (1,)), ((), ()))
TN = (((0,), (0,)), ((), ()))
NN = (((1,), (0,)), ((), ()))


def dot(a, b, dims=NN):
    return lax.dot_general(a, b, dims, preferred_element_type=F32)


def layer_kernel(
    late,
    tok_ref,
    cot_ref,
    ids_ref,
    wts_ref,
    gate_ref,
    up_ref,
    down_ref,
    tracker_ref,
    peer_ref,
    prev_ref,
    out_ref,
    new_ref,
    stage,
    spread,
    rows,
    weights,
    gu,
    hd,
    gug,
    wtd,
    part,
    grads,
    gsend,
    grecv,
    psend,
    precv,
    ret,
    zsend,
    msend,
    mrecv,
    kept,
    z_ss,
    z_rs,
    a_ss,
    a_rs,
    w_ss,
    w_rs,
    g_ss,
    g_rs,
    p_ss,
    p_rs,
    r_ss,
    r_rs,
    m_ss,
    m_rs,
    own_sem,
    kept_sem,
):
    rep = lax.axis_index("rep")
    e = lax.axis_index("exp")
    z = e // 4
    x = e - 4 * z
    odd = x % 2
    pair = e + 1 - 2 * odd
    mate = 4 * z + (x + 3 + 2 * odd) % 4

    def at_z(d):
        return 4 * ((z + d) % 4) + x

    def across(bit):
        step = 2**bit
        return rep + step * (1 - 2 * ((rep // step) % 2))

    def send(src, dst, ss, rs, to, replica=None):
        return pltpu.make_async_remote_copy(
            src_ref=src,
            dst_ref=dst,
            send_sem=ss,
            recv_sem=rs,
            device_id=(rep if replica is None else replica, to),
            device_id_type=pl.DeviceIdType.MESH,
        )

    own = [
        pltpu.make_async_copy(ref, weights.at[0, pl.ds(i * HID, HID)], own_sem.at[i])
        for i, ref in enumerate((gate_ref, up_ref, down_ref))
    ]
    keep = [
        pltpu.make_async_copy(ref, kept.at[i], kept_sem.at[i])
        for i, ref in enumerate((tracker_ref, peer_ref, prev_ref))
    ]
    barrier = pltpu.get_barrier_semaphore()
    peers = [(rep, at_z(1)), (rep, at_z(2)), (rep, at_z(3)), (rep, pair), (rep, mate)]
    peers += [(across(bit), e) for bit in late]
    for to in peers:
        pl.semaphore_signal(
            barrier, inc=1, device_id=to, device_id_type=pl.DeviceIdType.MESH
        )
    for copy in own:
        copy.start()

    lane = lax.broadcasted_iota(jnp.int32, (TOK, TOK), 1)
    sub = lax.broadcasted_iota(jnp.int32, (TOK, TOK), 0)
    before = (sub < lane).astype(F32).astype(BF16)
    expert = lax.broadcasted_iota(jnp.int32, (8, TOK), 0)
    slot = lax.broadcasted_iota(jnp.int32, (CAP, TOK), 0).astype(F32)
    ids = ids_ref[...]
    wts = wts_ref[...].astype(F32)
    hit0 = (expert == ids[0:1]).astype(F32)
    hit1 = (expert == ids[1:2]).astype(F32)
    hit_t = hit0 + hit1
    coef_t = hit0 * wts[0:1] + hit1 * wts[1:2]
    rank_t = dot(hit_t.astype(BF16), before)

    def place(d):
        mine = expert == (z + d) % 4
        zero = jnp.zeros((8, TOK), F32)
        hit = jnp.sum(jnp.where(mine, hit_t, zero), axis=0, keepdims=True)
        rank = jnp.sum(jnp.where(mine, rank_t, zero), axis=0, keepdims=True)
        coef = jnp.sum(jnp.where(mine, coef_t, zero), axis=0, keepdims=True)
        placed = jnp.where(slot == rank, 1.0, 0.0) * hit
        plain = placed.astype(BF16)
        spread[pl.ds(pl.multiple_of(d * CAP, 16), CAP)] = plain
        t = dot(plain, tok_ref[...]).astype(BF16)
        c = dot((placed * coef).astype(BF16), cot_ref[...]).astype(BF16)
        return t, c

    def w_copy(i):
        piece = pl.ds(i * HID, HID)
        return send(weights.at[0, piece], weights.at[1, piece], w_ss.at[i], w_rs.at[i], mate)

    def z_copy(d):
        return send(stage.at[d], rows.at[0, :, z], z_ss.at[d], z_rs.at[d], at_z(d))

    def z_arrive(d):
        return send(stage.at[d], rows.at[0, :, (z + 4 - d) % 4], z_ss.at[d], z_rs.at[d], at_z(d))

    def a_copy(d):
        zs = (z + 4 - d) % 4
        return send(rows.at[0, :, zs], rows.at[1, :, zs], a_ss.at[d], a_rs.at[d], pair)

    pl.semaphore_wait(barrier, len(peers))
    for i in range(2):
        own[i].wait()
        w_copy(i).start()
    def place_step(i, carry):
        d = (2 * i + 1 - i // 2) % 4
        t, c = place(d)

        @pl.when(d == 0)
        def _():
            rows[0, 0, z] = t
            rows[0, 1, z] = c
            a_copy(0).start()

        @pl.when(d != 0)
        def _():
            stage[d, 0] = t
            stage[d, 1] = c

        @pl.when(i < 2)
        def _():
            z_copy(d).start()

        return carry

    lax.fori_loop(0, 4, place_step, 0)
    own[2].wait()
    for copy in keep:
        copy.start()

    z_copy(1).wait_send()
    z_copy(3).wait_send()
    z_copy(2).start()
    for d in ORDER:
        if d == 2:
            w_copy(0).wait_send()
            w_copy(1).wait_send()
            w_copy(2).start()
        z_arrive(d).wait_recv()
        a_copy(d).start()

    def chunk(c):
        return pl.ds(CHUNKS[c][0], CHUNKS[c][1])

    def g_copy(c):
        at = chunk(c)
        return send(gsend.at[at], grecv.at[at], g_ss.at[c], g_rs.at[c], mate)

    def m_copy(i, c):
        at = chunk(c)
        return send(
            msend.at[i, at], mrecv.at[i, at], m_ss.at[i, c], m_rs.at[i, c], e, across(late[i])
        )

    def each_tile(start, count, step, body):
        def run(i, carry):
            body(pl.ds(pl.multiple_of(start + i * step, 16), step))
            return carry

        lax.fori_loop(0, count, run, 0)

    def grad_step(n, carry):
        rg = n // 2
        hs = (n + rg) % 2

        @pl.when(n == 1)
        def _():
            w_copy(0).wait_recv()
            w_copy(1).wait_recv()

        @pl.when(n == 2)
        def _():
            for d in range(4):
                a_copy(d).wait_recv()

        def project(i, carry):
            piece = pl.ds(pl.multiple_of(i * HID, 16), HID)
            gu[2 * rg + hs, piece] = dot(weights[hs, piece], rows[rg, 0].reshape(COLS, D), NT)
            return carry

        lax.fori_loop(0, 2, project, 0)

        def body(at):
            g = gu[2 * rg + hs, at]
            u = gu[2 * rg + hs, pl.ds(at.start + HID, at.size)]
            wtd[at] = (g * jax.nn.sigmoid(g) * u).astype(BF16)

        each_tile(0, HID // 32, 32, body)
        def accumulate(i, carry):
            at = pl.ds(pl.multiple_of(i * WIDE, WIDE), WIDE)
            share = dot(wtd[...], rows[rg, 1, :, :, at].reshape(COLS, WIDE))

            @pl.when(n < 2)
            def _():
                grads[hs, :, at] = share

            @pl.when(n >= 2)
            def _():
                grads[hs, :, at] += share

            return carry

        lax.fori_loop(0, D // WIDE, accumulate, 0)

        @pl.when(n == 2)
        def _():
            def ready(at):
                gsend[at] = grads[1, at].astype(BF16)

            each_tile(0, HID // 16, 16, ready)
            g_copy(0).start()
            g_copy(1).start()

        return carry

    lax.fori_loop(0, 4, grad_step, 0)
    for copy in keep:
        copy.wait()

    def begin(at):
        share = (grads[0, at] + grecv[at].astype(F32) - kept[2, at].astype(F32)) / ROUNDS
        mixed = (kept[0, at].astype(F32) + kept[1, at].astype(F32)) * 0.5
        mixed = mixed + (share if len(late) == 2 else 2.0 * share)
        grads[0, at] = share
        grads[1, at] = mixed
        msend[0, at] = mixed.astype(BF16)

    for c, (start, size) in enumerate(CHUNKS):
        if c + 2 < len(CHUNKS):
            g_copy(c).wait_send()
            g_copy(c + 2).start()
        g_copy(c).wait_recv()
        each_tile(start, size // 16, 16, begin)
        m_copy(0, c).start()

    def mixed_by(i, at):
        return (grads[1, at] + mrecv[i, at].astype(F32)) * 0.5 + grads[0, at]

    def pass_on():
        def body(at):
            mixed = mixed_by(0, at)
            grads[1, at] = mixed
            msend[1, at] = mixed.astype(BF16)

        for c, (start, size) in enumerate(CHUNKS):
            m_copy(0, c).wait_recv()
            each_tile(start, size // 16, 16, body)
            m_copy(1, c).start()

    if len(late) == 2 and late[0] == 0:
        pass_on()

    def p_copy(d):
        zs = (z + d) % 4
        return send(psend.at[zs], precv.at[zs], p_ss.at[d], p_rs.at[d], pair)

    w_copy(2).wait_recv()

    def input_step(n, carry):
        rg = 1 - n // 2
        hs = n % 2
        hd[...] = dot(weights[hs, 2 * HID:3 * HID], rows[rg, 1].reshape(COLS, D), NT)

        def body(at):
            low = pl.ds(at.start + HID, at.size)
            g = gu[2 * rg + hs, at]
            u = gu[2 * rg + hs, low]
            h = hd[at]
            s = jax.nn.sigmoid(g)
            gug[at] = (h * u * s * (1.0 + g * (1.0 - s))).astype(BF16)
            gug[low] = (h * (g * s)).astype(BF16)

        each_tile(0, HID // 32, 32, body)
        def accumulate(i, carry):
            at = pl.ds(pl.multiple_of(i * WIDE, WIDE), WIDE)
            share = dot(gug[...], weights[hs, 0:2 * HID, at], TN)

            @pl.when(hs == 0)
            def _():
                part[:, at] = share

            @pl.when(hs == 1)
            def _():
                part[:, at] += share

            return carry

        lax.fori_loop(0, D // WIDE, accumulate, 0)

        @pl.when(n == 1)
        def _():
            def ready(at):
                psend[(at.start // CAP), pl.ds(at.start % CAP, 16)] = part[at].astype(BF16)

            each_tile(0, COLS // 16, 16, ready)
            p_copy(2).start()
            p_copy(1).start()

        return carry

    lax.fori_loop(0, 4, input_step, 0)
    p_copy(2).wait_send()
    p_copy(3).start()
    p_copy(1).wait_send()
    p_copy(0).start()

    def r_copy(d):
        return send(zsend.at[d], ret.at[4 - d], r_ss.at[d], r_rs.at[4 - d], at_z(d))

    for d in (2, 1, 3, 0):
        p_copy(d).wait_recv()
        zs = (z + d) % 4
        to = ret if d == 0 else zsend

        def add(at):
            mine = part[pl.ds(pl.multiple_of(zs * CAP + at.start, 16), 16)]
            to[d, at] = (mine + precv[zs, at].astype(F32)).astype(BF16)

        each_tile(0, CAP // 16, 16, add)
        if d != 0:
            r_copy(d).start()

    if len(late) == 2 and late[0] != 0:
        pass_on()
    for d in (1, 3, 2):
        r_copy(d).wait_recv()

    def collect(i, carry):
        at = pl.ds(pl.multiple_of(i * WIDE, WIDE), WIDE)
        found = dot(spread[...], ret[:, :, at].reshape(COLS, WIDE), TN)
        out_ref[:, at] = found.astype(BF16)
        return carry

    lax.fori_loop(0, D // WIDE, collect, 0)
    last = len(late) - 1

    def finish(at):
        new_ref[at] = mixed_by(last, at).astype(BF16)

    for c, (start, size) in enumerate(CHUNKS):
        m_copy(last, c).wait_recv()
        each_tile(start, size // 16, 16, finish)

    z_copy(2).wait_send()
    p_copy(3).wait_send()
    p_copy(0).wait_send()
    for d in (1, 2, 3):
        r_copy(d).wait_send()
    for d in range(4):
        a_copy(d).wait_send()
    w_copy(2).wait_send()
    for c in range(len(CHUNKS)):
        if c >= len(CHUNKS) - 2:
            g_copy(c).wait_send()
        for i in range(len(late)):
            m_copy(i, c).wait_send()


def layer(late, number, *arrays):
    vmem = pl.BlockSpec(memory_space=pltpu.VMEM)
    hbm = pl.BlockSpec(memory_space=pl.ANY)
    dma = pltpu.SemaphoreType.DMA
    return pl.pallas_call(
        partial(layer_kernel, late),
        out_shape=(
            jax.ShapeDtypeStruct((TOK, D), BF16),
            jax.ShapeDtypeStruct((HID, D), BF16),
        ),
        in_specs=[vmem] * 4 + [hbm] * 6,
        out_specs=(vmem, vmem),
        scratch_shapes=[
            pltpu.VMEM((4, 2, CAP, D), BF16),
            pltpu.VMEM((COLS, TOK), BF16),
            pltpu.VMEM((2, 2, 4, CAP, D), BF16),
            pltpu.VMEM((2, 3 * HID, D), BF16),
            pltpu.VMEM((4, 2 * HID, COLS), F32),
            pltpu.VMEM((HID, COLS), F32),
            pltpu.VMEM((2 * HID, COLS), BF16),
            pltpu.VMEM((HID, COLS), BF16),
            pltpu.VMEM((COLS, D), F32),
            pltpu.VMEM((2, HID, D), F32),
            pltpu.VMEM((HID, D), BF16),
            pltpu.VMEM((HID, D), BF16),
            pltpu.VMEM((4, CAP, D), BF16),
            pltpu.VMEM((4, CAP, D), BF16),
            pltpu.VMEM((4, CAP, D), BF16),
            pltpu.VMEM((4, CAP, D), BF16),
            pltpu.VMEM((len(late), HID, D), BF16),
            pltpu.VMEM((len(late), HID, D), BF16),
            pltpu.VMEM((3, HID, D), BF16),
            dma((4,)),
            dma((4,)),
            dma((4,)),
            dma((4,)),
            dma((3,)),
            dma((3,)),
            dma((len(CHUNKS),)),
            dma((len(CHUNKS),)),
            dma((4,)),
            dma((4,)),
            dma((4,)),
            dma((4,)),
            dma((len(late), len(CHUNKS))),
            dma((len(late), len(CHUNKS))),
            dma((3,)),
            dma((3,)),
        ],
        compiler_params=pltpu.CompilerParams(
            collective_id=number, has_side_effects=True, vmem_limit_bytes=56 * 2**20
        ),
        cost_estimate=pl.CostEstimate(
            flops=7 * 10**9, bytes_accessed=6 * 10**6, transcendentals=10**6
        ),
    )(*arrays)


def from_peer(state, bit):
    count = lax.axis_size("rep")
    pairs = [(source, source ^ (1 << bit)) for source in range(count)]
    return lax.ppermute(state, "rep", pairs)


def shards(
    tokens,
    cotangent,
    route_ids,
    route_weights,
    gate_weight,
    up_weight,
    down_weight,
    tracker,
    grad_prev,
    gossip_step,
):
    steps = jnp.clip(gossip_step, 0, 2)[None, :]
    code = jnp.sum(steps * jnp.array([[9, 3, 1]], jnp.int32), axis=1, keepdims=True)
    found = code == jnp.arange(27, dtype=jnp.int32)[None, :]
    choice = jnp.sum(jnp.where(found, jnp.array(CHOICES, jnp.int32), 0), axis=1)
    choice = lax.optimization_barrier(choice)
    early, pick = choice[0], choice[1]
    maybe = [lambda state: state] + [partial(from_peer, bit=bit) for bit in range(3)]
    peer = lax.switch(early, maybe, tracker[0])
    out, new = lax.switch(
        pick,
        [partial(layer, late, number) for number, late in enumerate(LATE)],
        tokens[0],
        cotangent[0],
        route_ids[0].T,
        route_weights[0].T,
        gate_weight[0].T,
        up_weight[0].T,
        down_weight[0],
        tracker[0],
        peer,
        grad_prev[0],
    )
    return (out[None], new[None])


def solution(mesh):
    rows = P("rep", "exp", None)
    cols = P("rep", None, "exp")
    in_specs = (rows, rows, rows, rows, cols, cols, rows, rows, rows, P())
    return jax.shard_map(
        shards, mesh=mesh, in_specs=in_specs, out_specs=(rows, rows), check_vma=False
    )
```

```python
from functools import partial

import jax
import jax.numpy as jnp
from jax import lax
from jax.experimental import pallas as pl
from jax.experimental.pallas import tpu as pltpu
from jax.sharding import PartitionSpec as P

D = 1024
EXPERTS = 4
ROUNDS = 3
TOK = 128
CAP = 96
WIDE = 256
HID = 352
COLS = 4 * CAP
ORDER = (1, 3, 2)
CHUNKS = ((0, 96), (96, 80), (176, 96), (272, 80))
HALF = HID // 2
LATE = ((0,), (1,), (2,), (0, 1), (0, 2), (1, 0), (1, 2), (2, 0), (2, 1))
F32 = jnp.float32
BF16 = jnp.bfloat16
NT = (((1,), (1,)), ((), ()))
TN = (((0,), (0,)), ((), ()))
NN = (((1,), (0,)), ((), ()))


def dot(a, b, dims=NN):
    return lax.dot_general(a, b, dims, preferred_element_type=F32)


def layer_kernel(
    late,
    tok_ref,
    cot_ref,
    ids_ref,
    wts_ref,
    gate_ref,
    up_ref,
    down_ref,
    start_ref,
    prev_ref,
    out_ref,
    new_ref,
    stage,
    spread,
    rows,
    weights,
    gu,
    hd,
    gug,
    wtd,
    part,
    grads,
    gsend,
    grecv,
    psend,
    precv,
    ret,
    zsend,
    msend,
    mrecv,
    kept,
    z_ss,
    z_rs,
    a_ss,
    a_rs,
    w_ss,
    w_rs,
    g_ss,
    g_rs,
    p_ss,
    p_rs,
    r_ss,
    r_rs,
    m_ss,
    m_rs,
    own_sem,
    kept_sem,
):
    rep = lax.axis_index("rep")
    e = lax.axis_index("exp")
    z = e // 4
    x = e - 4 * z
    odd = x % 2
    pair = e + 1 - 2 * odd
    mate = 4 * z + (x + 3 + 2 * odd) % 4

    def at_z(d):
        return 4 * ((z + d) % 4) + x

    def across(*bits):
        return rep + sum(2**bit * (1 - 2 * ((rep // 2**bit) % 2)) for bit in bits)

    hops = [across(bit) for bit in late]
    if late == (2, 1):
        hops[0] = across(1, 2)
    halves = len(late) == 2 and late[1] == 0

    def send(src, dst, ss, rs, to, replica=None):
        return pltpu.make_async_remote_copy(
            src_ref=src,
            dst_ref=dst,
            send_sem=ss,
            recv_sem=rs,
            device_id=(rep if replica is None else replica, to),
            device_id_type=pl.DeviceIdType.MESH,
        )

    own = [
        pltpu.make_async_copy(ref, weights.at[0, pl.ds(i * HID, HID)], own_sem.at[i])
        for i, ref in enumerate((gate_ref, up_ref, down_ref))
    ]
    keep = [
        pltpu.make_async_copy(ref, kept.at[i], kept_sem.at[i])
        for i, ref in enumerate((start_ref, prev_ref))
    ]
    barrier = pltpu.get_barrier_semaphore()
    peers = [(rep, at_z(1)), (rep, at_z(2)), (rep, at_z(3)), (rep, pair), (rep, mate)]
    peers += [(hop, e) for hop in hops]
    for to in peers:
        pl.semaphore_signal(
            barrier, inc=1, device_id=to, device_id_type=pl.DeviceIdType.MESH
        )
    for copy in own:
        copy.start()

    lane = lax.broadcasted_iota(jnp.int32, (TOK, TOK), 1)
    sub = lax.broadcasted_iota(jnp.int32, (TOK, TOK), 0)
    before = (sub < lane).astype(F32).astype(BF16)
    expert = lax.broadcasted_iota(jnp.int32, (8, TOK), 0)
    slot = lax.broadcasted_iota(jnp.int32, (CAP, TOK), 0).astype(F32)
    ids = ids_ref[...]
    wts = wts_ref[...].astype(F32)
    hit0 = (expert == ids[0:1]).astype(F32)
    hit1 = (expert == ids[1:2]).astype(F32)
    hit_t = hit0 + hit1
    coef_t = hit0 * wts[0:1] + hit1 * wts[1:2]
    rank_t = dot(hit_t.astype(BF16), before)

    def place(d):
        mine = expert == (z + d) % 4
        zero = jnp.zeros((8, TOK), F32)
        hit = jnp.sum(jnp.where(mine, hit_t, zero), axis=0, keepdims=True)
        rank = jnp.sum(jnp.where(mine, rank_t, zero), axis=0, keepdims=True)
        coef = jnp.sum(jnp.where(mine, coef_t, zero), axis=0, keepdims=True)
        placed = jnp.where(slot == rank, 1.0, 0.0) * hit
        plain = placed.astype(BF16)
        spread[pl.ds(pl.multiple_of(d * CAP, 16), CAP)] = plain
        t = dot(plain, tok_ref[...]).astype(BF16)
        c = dot((placed * coef).astype(BF16), cot_ref[...]).astype(BF16)
        return t, c

    def w_copy(i):
        piece = pl.ds(i * HID, HID)
        return send(weights.at[0, piece], weights.at[1, piece], w_ss.at[i], w_rs.at[i], mate)

    def z_copy(d):
        return send(stage.at[d], rows.at[0, :, z], z_ss.at[d], z_rs.at[d], at_z(d))

    def z_arrive(d):
        return send(stage.at[d], rows.at[0, :, (z + 4 - d) % 4], z_ss.at[d], z_rs.at[d], at_z(d))

    def a_copy(d):
        zs = (z + 4 - d) % 4
        return send(rows.at[0, :, zs], rows.at[1, :, zs], a_ss.at[d], a_rs.at[d], pair)

    pl.semaphore_wait(barrier, len(peers))
    for i in range(2):
        own[i].wait()
        w_copy(i).start()
    def place_step(i, carry):
        d = (2 * i + 1 - i // 2) % 4
        t, c = place(d)

        @pl.when(d == 0)
        def _():
            rows[0, 0, z] = t
            rows[0, 1, z] = c
            a_copy(0).start()

        @pl.when(d != 0)
        def _():
            stage[d, 0] = t
            stage[d, 1] = c

        @pl.when(i < 2)
        def _():
            z_copy(d).start()

        return carry

    lax.fori_loop(0, 4, place_step, 0)
    own[2].wait()
    for copy in keep:
        copy.start()

    z_copy(1).wait_send()
    z_copy(3).wait_send()
    z_copy(2).start()
    for d in ORDER:
        if d == 2:
            w_copy(0).wait_send()
            w_copy(1).wait_send()
            w_copy(2).start()
        z_arrive(d).wait_recv()
        a_copy(d).start()

    def chunk(c):
        return pl.ds(CHUNKS[c][0], CHUNKS[c][1])

    def g_copy(c):
        at = chunk(c)
        return send(gsend.at[at], grecv.at[at], g_ss.at[c], g_rs.at[c], mate)

    def m_copy(i, c):
        at = chunk(c)
        return send(
            msend.at[i, at],
            mrecv.at[i, at],
            m_ss.at[i, c],
            m_rs.at[i, c],
            e,
            hops[1] if halves else hops[i],
        )

    def half_copy(j, passed, core):
        at = pl.ds(pl.multiple_of(core * HALF + CHUNKS[j][0], 16), CHUNKS[j][1])
        k = 2 * passed + j
        source = mrecv if passed else msend
        return send(
            source.at[2, at], mrecv.at[2, at], m_ss.at[2, k], m_rs.at[2, k], e, hops[passed]
        )

    def each_tile(start, count, step, body):
        def run(i, carry):
            body(pl.ds(pl.multiple_of(start + i * step, 16), step))
            return carry

        lax.fori_loop(0, count, run, 0)

    def grad_step(n, carry):
        rg = n // 2
        hs = (n + rg) % 2

        @pl.when(n == 1)
        def _():
            w_copy(0).wait_recv()
            w_copy(1).wait_recv()

        @pl.when(n == 2)
        def _():
            for d in range(4):
                a_copy(d).wait_recv()

        def project(i, carry):
            piece = pl.ds(pl.multiple_of(i * HID, 16), HID)
            gu[2 * rg + hs, piece] = dot(weights[hs, piece], rows[rg, 0].reshape(COLS, D), NT)
            return carry

        lax.fori_loop(0, 2, project, 0)

        def body(at):
            g = gu[2 * rg + hs, at]
            u = gu[2 * rg + hs, pl.ds(at.start + HID, at.size)]
            wtd[at] = (g * jax.nn.sigmoid(g) * u).astype(BF16)

        each_tile(0, HID // 32, 32, body)
        def accumulate(i, carry):
            at = pl.ds(pl.multiple_of(i * WIDE, WIDE), WIDE)
            share = dot(wtd[...], rows[rg, 1, :, :, at].reshape(COLS, WIDE))

            @pl.when(n < 2)
            def _():
                grads[hs, :, at] = share

            @pl.when(n >= 2)
            def _():
                grads[hs, :, at] += share

            return carry

        lax.fori_loop(0, D // WIDE, accumulate, 0)

        @pl.when(n == 2)
        def _():
            def ready(at):
                gsend[at] = grads[1, at].astype(BF16)

            each_tile(0, HID // 16, 16, ready)
            g_copy(0).start()
            g_copy(1).start()

        return carry

    lax.fori_loop(0, 4, grad_step, 0)
    for copy in keep:
        copy.wait()

    def begin(at):
        share = (grads[0, at] + grecv[at].astype(F32) - kept[1, at].astype(F32)) / ROUNDS
        mixed = kept[0, at].astype(F32) + (share if len(late) == 2 else 2.0 * share)
        grads[0, at] = share
        grads[1, at] = mixed
        msend[0, at] = mixed.astype(BF16)
        if halves:
            msend[1, at] = share.astype(BF16)

    for c, (start, size) in enumerate(CHUNKS):
        if c + 2 < len(CHUNKS):
            g_copy(c).wait_send()
            g_copy(c + 2).start()
        g_copy(c).wait_recv()
        each_tile(start, size // 16, 16, begin)
        m_copy(0, c).start()
        if halves:
            m_copy(1, c).start()

    def mixed_by(i, at):
        return (grads[1, at] + mrecv[i, at].astype(F32)) * 0.5 + grads[0, at]

    def pass_on():
        def body(at):
            mixed = mixed_by(0, at)
            grads[1, at] = mixed
            msend[1, at] = mixed.astype(BF16)

        for c, (start, size) in enumerate(CHUNKS):
            m_copy(0, c).wait_recv()
            each_tile(start, size // 16, 16, body)
            m_copy(1, c).start()

    core = rep % 2

    def meet(at):
        mixed = (grads[1, at] + mrecv[0, at].astype(F32)) * 0.5
        grads[0, at] = 1.5 * grads[0, at] + 0.5 * mrecv[1, at].astype(F32)
        grads[1, at] = mixed
        msend[2, at] = mixed.astype(BF16)

    if halves:
        for c, (start, size) in enumerate(CHUNKS):
            m_copy(0, c).wait_recv()
            m_copy(1, c).wait_recv()
            each_tile(start, size // 16, 16, meet)
        for j in range(2):
            half_copy(j, 0, core).start()
    elif len(late) == 2 and late[0] == 0:
        pass_on()

    def p_copy(d):
        zs = (z + d) % 4
        return send(psend.at[zs], precv.at[zs], p_ss.at[d], p_rs.at[d], pair)

    w_copy(2).wait_recv()

    def input_step(n, carry):
        rg = 1 - n // 2
        hs = n % 2
        hd[...] = dot(weights[hs, 2 * HID:3 * HID], rows[rg, 1].reshape(COLS, D), NT)

        def body(at):
            low = pl.ds(at.start + HID, at.size)
            g = gu[2 * rg + hs, at]
            u = gu[2 * rg + hs, low]
            h = hd[at]
            s = jax.nn.sigmoid(g)
            gug[at] = (h * u * s * (1.0 + g * (1.0 - s))).astype(BF16)
            gug[low] = (h * (g * s)).astype(BF16)

        each_tile(0, HID // 32, 32, body)
        def accumulate(i, carry):
            at = pl.ds(pl.multiple_of(i * WIDE, WIDE), WIDE)
            share = dot(gug[...], weights[hs, 0:2 * HID, at], TN)

            @pl.when(hs == 0)
            def _():
                part[:, at] = share

            @pl.when(hs == 1)
            def _():
                part[:, at] += share

            return carry

        lax.fori_loop(0, D // WIDE, accumulate, 0)

        @pl.when(n == 1)
        def _():
            def ready(at):
                psend[(at.start // CAP), pl.ds(at.start % CAP, 16)] = part[at].astype(BF16)

            each_tile(0, COLS // 16, 16, ready)
            p_copy(2).start()
            p_copy(1).start()

        return carry

    lax.fori_loop(0, 4, input_step, 0)
    p_copy(2).wait_send()
    p_copy(3).start()
    p_copy(1).wait_send()
    p_copy(0).start()

    def r_copy(d):
        return send(zsend.at[d], ret.at[4 - d], r_ss.at[d], r_rs.at[4 - d], at_z(d))

    for d in (2, 1, 3, 0):
        p_copy(d).wait_recv()
        zs = (z + d) % 4
        to = ret if d == 0 else zsend

        def add(at):
            mine = part[pl.ds(pl.multiple_of(zs * CAP + at.start, 16), 16)]
            to[d, at] = (mine + precv[zs, at].astype(F32)).astype(BF16)

        each_tile(0, CAP // 16, 16, add)
        if d != 0:
            r_copy(d).start()

    if halves:
        for j in range(2):
            half_copy(j, 0, core).wait_recv()
            half_copy(j, 1, core).start()
    elif len(late) == 2 and late[0] != 0:
        pass_on()
    for d in (1, 3, 2):
        r_copy(d).wait_recv()

    def collect(i, carry):
        at = pl.ds(pl.multiple_of(i * WIDE, WIDE), WIDE)
        found = dot(spread[...], ret[:, :, at].reshape(COLS, WIDE), TN)
        out_ref[:, at] = found.astype(BF16)
        return carry

    lax.fori_loop(0, D // WIDE, collect, 0)
    last = 2 if halves else len(late) - 1
    if halves:
        for j in range(2):
            half_copy(j, 1, 1 - core).wait_recv()

    def finish(at):
        new_ref[at] = mixed_by(last, at).astype(BF16)

    for c, (start, size) in enumerate(CHUNKS):
        if not halves:
            m_copy(last, c).wait_recv()
        each_tile(start, size // 16, 16, finish)

    z_copy(2).wait_send()
    p_copy(3).wait_send()
    p_copy(0).wait_send()
    for d in (1, 2, 3):
        r_copy(d).wait_send()
    for d in range(4):
        a_copy(d).wait_send()
    w_copy(2).wait_send()
    if halves:
        for j in range(2):
            half_copy(j, 0, core).wait_send()
            half_copy(j, 1, core).wait_send()
    for c in range(len(CHUNKS)):
        if c >= len(CHUNKS) - 2:
            g_copy(c).wait_send()
        for i in range(len(late)):
            m_copy(i, c).wait_send()


def layer(late, number, *arrays):
    vmem = pl.BlockSpec(memory_space=pltpu.VMEM)
    hbm = pl.BlockSpec(memory_space=pl.ANY)
    dma = pltpu.SemaphoreType.DMA
    slots = 3 if len(late) == 2 and late[1] == 0 else len(late)
    return pl.pallas_call(
        partial(layer_kernel, late),
        out_shape=(
            jax.ShapeDtypeStruct((TOK, D), BF16),
            jax.ShapeDtypeStruct((HID, D), BF16),
        ),
        in_specs=[vmem] * 4 + [hbm] * 5,
        out_specs=(vmem, vmem),
        scratch_shapes=[
            pltpu.VMEM((4, 2, CAP, D), BF16),
            pltpu.VMEM((COLS, TOK), BF16),
            pltpu.VMEM((2, 2, 4, CAP, D), BF16),
            pltpu.VMEM((2, 3 * HID, D), BF16),
            pltpu.VMEM((4, 2 * HID, COLS), F32),
            pltpu.VMEM((HID, COLS), F32),
            pltpu.VMEM((2 * HID, COLS), BF16),
            pltpu.VMEM((HID, COLS), BF16),
            pltpu.VMEM((COLS, D), F32),
            pltpu.VMEM((2, HID, D), F32),
            pltpu.VMEM((HID, D), BF16),
            pltpu.VMEM((HID, D), BF16),
            pltpu.VMEM((4, CAP, D), BF16),
            pltpu.VMEM((4, CAP, D), BF16),
            pltpu.VMEM((4, CAP, D), BF16),
            pltpu.VMEM((4, CAP, D), BF16),
            pltpu.VMEM((slots, HID, D), BF16),
            pltpu.VMEM((slots, HID, D), BF16),
            pltpu.VMEM((2, HID, D), BF16),
            dma((4,)),
            dma((4,)),
            dma((4,)),
            dma((4,)),
            dma((3,)),
            dma((3,)),
            dma((len(CHUNKS),)),
            dma((len(CHUNKS),)),
            dma((4,)),
            dma((4,)),
            dma((4,)),
            dma((4,)),
            dma((slots, len(CHUNKS))),
            dma((slots, len(CHUNKS))),
            dma((3,)),
            dma((3,)),
        ],
        compiler_params=pltpu.CompilerParams(
            collective_id=number, has_side_effects=True, vmem_limit_bytes=56 * 2**20
        ),
        cost_estimate=pl.CostEstimate(
            flops=7 * 10**9, bytes_accessed=6 * 10**6, transcendentals=10**6
        ),
    )(*arrays)


def from_peer(state, bit):
    count = lax.axis_size("rep")
    pairs = [(source, source ^ (1 << bit)) for source in range(count)]
    return lax.ppermute(state, "rep", pairs)


def average(state, bit):
    peer = from_peer(state, bit)
    return ((state.astype(F32) + peer.astype(F32)) * 0.5).astype(BF16)


def average_with_core(state, bit):
    state = average(state, 0)
    first = lax.axis_index("rep") % 2 == 0
    top, low = state[:HALF], state[HALF:]
    mine = from_peer(jnp.where(first, top, low), bit)
    other = from_peer(mine, 0)
    peer = jnp.where(first, jnp.stack([mine, other]), jnp.stack([other, mine]))
    peer = peer.reshape(state.shape)
    return ((state.astype(F32) + peer.astype(F32)) * 0.5).astype(BF16)


def shards(
    tokens,
    cotangent,
    route_ids,
    route_weights,
    gate_weight,
    up_weight,
    down_weight,
    tracker,
    grad_prev,
    gossip_step,
):
    steps = jnp.clip(gossip_step, 0, 2)
    place = lax.broadcasted_iota(jnp.int32, (3,), 0)
    code = jnp.sum(steps * jnp.where(place == 0, 9, jnp.where(place == 1, 3, 1)), keepdims=True)
    number = lax.broadcasted_iota(jnp.int32, (2, 32), 1)
    s1, s2, s3 = number // 9, number // 3 % 3, number % 3
    early = jnp.where((s1 == s2) | (s1 == s3), 0, s1 + 1)
    early = jnp.where((early > 1) & ((s2 == 0) | (s3 == 0)), early + 2, early)
    pick = jnp.where(s2 == s3, s2, 3 + 2 * s2 + jnp.where(s3 > s2, s3 - 1, s3))
    table = jnp.where(lax.broadcasted_iota(jnp.int32, (2, 32), 0) == 0, early, pick)
    choice = jnp.sum(jnp.where(number == code, table, 0), axis=1)
    choice = lax.optimization_barrier(choice)
    early, pick = choice[0], choice[1]
    maybe = [lambda state: state] + [partial(average, bit=bit) for bit in range(3)]
    maybe += [partial(average_with_core, bit=bit) for bit in (1, 2)]
    start = lax.switch(early, maybe, tracker[0])
    out, new = lax.switch(
        pick,
        [partial(layer, late, number) for number, late in enumerate(LATE)],
        tokens[0],
        cotangent[0],
        route_ids[0].T,
        route_weights[0].T,
        gate_weight[0].T,
        up_weight[0].T,
        down_weight[0],
        start,
        grad_prev[0],
    )
    return (out[None], new[None])


def solution(mesh):
    rows = P("rep", "exp", None)
    cols = P("rep", None, "exp")
    in_specs = (rows, rows, rows, rows, cols, cols, rows, rows, rows, P())
    return jax.shard_map(
        shards, mesh=mesh, in_specs=in_specs, out_specs=(rows, rows), check_vma=False
    )
```

```python
from functools import partial

import jax
import jax.numpy as jnp
from jax import lax
from jax.experimental import pallas as pl
from jax.experimental.pallas import tpu as pltpu
from jax.sharding import PartitionSpec as P

D = 1024
EXPERTS = 4
ROUNDS = 3
TOK = 128
CAP = 96
WIDE = 256
HID = 352
COLS = 4 * CAP
ORDER = (1, 3, 2)
CHUNKS = ((0, 96), (96, 80), (176, 96), (272, 80))
HALF = HID // 2
LATE = ((0,), (1,), (2,), (0, 1), (0, 2), (1, 0), (1, 2), (2, 0), (2, 1))
F32 = jnp.float32
BF16 = jnp.bfloat16
NT = (((1,), (1,)), ((), ()))
TN = (((0,), (0,)), ((), ()))
NN = (((1,), (0,)), ((), ()))


def dot(a, b, dims=NN):
    return lax.dot_general(a, b, dims, preferred_element_type=F32)


def layer_kernel(
    late,
    tok_ref,
    cot_ref,
    ids_ref,
    wts_ref,
    gate_ref,
    up_ref,
    down_ref,
    start_ref,
    prev_ref,
    out_ref,
    new_ref,
    stage,
    spread,
    rows,
    weights,
    gu,
    hd,
    gug,
    wtd,
    part,
    grads,
    gsend,
    grecv,
    psend,
    precv,
    ret,
    zsend,
    msend,
    mrecv,
    kept,
    z_ss,
    z_rs,
    a_ss,
    a_rs,
    w_ss,
    w_rs,
    g_ss,
    g_rs,
    p_ss,
    p_rs,
    r_ss,
    r_rs,
    m_ss,
    m_rs,
    own_sem,
    kept_sem,
):
    rep = lax.axis_index("rep")
    e = lax.axis_index("exp")
    z = e // 4
    x = e - 4 * z
    odd = x % 2
    pair = e + 1 - 2 * odd
    mate = 4 * z + (x + 3 + 2 * odd) % 4

    def at_z(d):
        return 4 * ((z + d) % 4) + x

    def across(*bits):
        return rep + sum(2**bit * (1 - 2 * ((rep // 2**bit) % 2)) for bit in bits)

    hops = [across(bit) for bit in late]
    if late == (2, 1):
        hops[0] = across(1, 2)
    halves = len(late) == 2 and late[1] == 0

    def send(src, dst, ss, rs, to, replica=None):
        return pltpu.make_async_remote_copy(
            src_ref=src,
            dst_ref=dst,
            send_sem=ss,
            recv_sem=rs,
            device_id=(rep if replica is None else replica, to),
            device_id_type=pl.DeviceIdType.MESH,
        )

    own = [
        pltpu.make_async_copy(ref, weights.at[0, pl.ds(i * HID, HID)], own_sem.at[i])
        for i, ref in enumerate((gate_ref, up_ref, down_ref))
    ]
    keep = [
        pltpu.make_async_copy(ref, kept.at[i], kept_sem.at[i])
        for i, ref in enumerate((start_ref, prev_ref))
    ]
    barrier = pltpu.get_barrier_semaphore()
    peers = [(rep, at_z(1)), (rep, at_z(2)), (rep, at_z(3)), (rep, pair), (rep, mate)]
    peers += [(hop, e) for hop in hops]
    for to in peers:
        pl.semaphore_signal(
            barrier, inc=1, device_id=to, device_id_type=pl.DeviceIdType.MESH
        )
    for copy in own:
        copy.start()

    lane = lax.broadcasted_iota(jnp.int32, (TOK, TOK), 1)
    sub = lax.broadcasted_iota(jnp.int32, (TOK, TOK), 0)
    before = (sub < lane).astype(F32).astype(BF16)
    expert = lax.broadcasted_iota(jnp.int32, (8, TOK), 0)
    slot = lax.broadcasted_iota(jnp.int32, (CAP, TOK), 0).astype(F32)
    ids = ids_ref[...]
    wts = wts_ref[...].astype(F32)
    hit0 = (expert == ids[0:1]).astype(F32)
    hit1 = (expert == ids[1:2]).astype(F32)
    hit_t = hit0 + hit1
    coef_t = hit0 * wts[0:1] + hit1 * wts[1:2]
    rank_t = dot(hit_t.astype(BF16), before)

    def place(d):
        mine = expert == (z + d) % 4
        zero = jnp.zeros((8, TOK), F32)
        hit = jnp.sum(jnp.where(mine, hit_t, zero), axis=0, keepdims=True)
        rank = jnp.sum(jnp.where(mine, rank_t, zero), axis=0, keepdims=True)
        coef = jnp.sum(jnp.where(mine, coef_t, zero), axis=0, keepdims=True)
        placed = jnp.where(slot == rank, 1.0, 0.0) * hit
        plain = placed.astype(BF16)
        spread[pl.ds(pl.multiple_of(d * CAP, 16), CAP)] = plain
        t = dot(plain, tok_ref[...]).astype(BF16)
        c = dot((placed * coef).astype(BF16), cot_ref[...]).astype(BF16)
        return t, c

    def w_copy(i):
        piece = pl.ds(i * HID, HID)
        return send(weights.at[0, piece], weights.at[1, piece], w_ss.at[i], w_rs.at[i], mate)

    def z_copy(d):
        return send(stage.at[d], rows.at[0, :, z], z_ss.at[d], z_rs.at[d], at_z(d))

    def z_arrive(d):
        return send(stage.at[d], rows.at[0, :, (z + 4 - d) % 4], z_ss.at[d], z_rs.at[d], at_z(d))

    def a_copy(d):
        zs = (z + 4 - d) % 4
        return send(rows.at[0, :, zs], rows.at[1, :, zs], a_ss.at[d], a_rs.at[d], pair)

    pl.semaphore_wait(barrier, len(peers))
    for i in range(2):
        own[i].wait()
        w_copy(i).start()
    def place_step(i, carry):
        d = (2 * i + 1 - i // 2) % 4
        t, c = place(d)

        @pl.when(d == 0)
        def _():
            rows[0, 0, z] = t
            rows[0, 1, z] = c
            a_copy(0).start()

        @pl.when(d != 0)
        def _():
            stage[d, 0] = t
            stage[d, 1] = c

        @pl.when(i < 2)
        def _():
            z_copy(d).start()

        return carry

    lax.fori_loop(0, 4, place_step, 0)
    own[2].wait()
    for copy in keep:
        copy.start()

    z_copy(1).wait_send()
    z_copy(3).wait_send()
    z_copy(2).start()
    for d in ORDER:
        if d == 2:
            w_copy(0).wait_send()
            w_copy(1).wait_send()
            w_copy(2).start()
        z_arrive(d).wait_recv()
        a_copy(d).start()

    def chunk(c):
        return pl.ds(CHUNKS[c][0], CHUNKS[c][1])

    def g_copy(c):
        at = chunk(c)
        return send(gsend.at[at], grecv.at[at], g_ss.at[c], g_rs.at[c], mate)

    def m_copy(i, c):
        at = chunk(c)
        return send(
            msend.at[i, at],
            mrecv.at[i, at],
            m_ss.at[i, c],
            m_rs.at[i, c],
            e,
            hops[1] if halves else hops[i],
        )

    def half_copy(j, passed, core):
        at = pl.ds(pl.multiple_of(core * HALF + CHUNKS[j][0], 16), CHUNKS[j][1])
        k = 2 * passed + j
        source = mrecv if passed else msend
        return send(
            source.at[2, at], mrecv.at[2, at], m_ss.at[2, k], m_rs.at[2, k], e, hops[passed]
        )

    def each_tile(start, count, step, body):
        def run(i, carry):
            body(pl.ds(pl.multiple_of(start + i * step, 16), step))
            return carry

        lax.fori_loop(0, count, run, 0)

    def grad_step(n, carry):
        rg = n // 2
        hs = (n + rg) % 2

        @pl.when(n == 1)
        def _():
            w_copy(0).wait_recv()
            w_copy(1).wait_recv()

        @pl.when(n == 2)
        def _():
            for d in range(4):
                a_copy(d).wait_recv()

        def project(i, carry):
            piece = pl.ds(pl.multiple_of(i * HID, 16), HID)
            gu[2 * rg + hs, piece] = dot(weights[hs, piece], rows[rg, 0].reshape(COLS, D), NT)
            return carry

        lax.fori_loop(0, 2, project, 0)

        def body(at):
            g = gu[2 * rg + hs, at]
            u = gu[2 * rg + hs, pl.ds(at.start + HID, at.size)]
            wtd[at] = (g * jax.nn.sigmoid(g) * u).astype(BF16)

        each_tile(0, HID // 32, 32, body)
        def accumulate(i, carry):
            at = pl.ds(pl.multiple_of(i * WIDE, WIDE), WIDE)
            share = dot(wtd[...], rows[rg, 1, :, :, at].reshape(COLS, WIDE))

            @pl.when(n < 2)
            def _():
                grads[hs, :, at] = share

            @pl.when(n >= 2)
            def _():
                grads[hs, :, at] += share

            return carry

        lax.fori_loop(0, D // WIDE, accumulate, 0)

        @pl.when(n == 2)
        def _():
            def ready(at):
                gsend[at] = grads[1, at].astype(BF16)

            each_tile(0, HID // 16, 16, ready)
            g_copy(0).start()
            g_copy(1).start()

        return carry

    lax.fori_loop(0, 4, grad_step, 0)
    for copy in keep:
        copy.wait()

    def begin(at):
        share = (grads[0, at] + grecv[at].astype(F32) - kept[1, at].astype(F32)) / ROUNDS
        mixed = kept[0, at].astype(F32) + (share if len(late) == 2 else 2.0 * share)
        grads[0, at] = share
        grads[1, at] = mixed
        msend[0, at] = mixed.astype(BF16)
        if halves:
            msend[1, at] = share.astype(BF16)

    for c, (start, size) in enumerate(CHUNKS):
        if c + 2 < len(CHUNKS):
            g_copy(c).wait_send()
            g_copy(c + 2).start()
        g_copy(c).wait_recv()
        each_tile(start, size // 16, 16, begin)
        m_copy(0, c).start()
        if halves:
            m_copy(1, c).start()

    def mixed_by(i, at):
        return (grads[1, at] + mrecv[i, at].astype(F32)) * 0.5 + grads[0, at]

    def pass_on():
        def body(at):
            mixed = mixed_by(0, at)
            grads[1, at] = mixed
            msend[1, at] = mixed.astype(BF16)

        for c, (start, size) in enumerate(CHUNKS):
            m_copy(0, c).wait_recv()
            each_tile(start, size // 16, 16, body)
            m_copy(1, c).start()

    core = rep % 2

    def meet(at):
        mixed = (grads[1, at] + mrecv[0, at].astype(F32)) * 0.5
        grads[0, at] = 1.5 * grads[0, at] + 0.5 * mrecv[1, at].astype(F32)
        grads[1, at] = mixed
        msend[2, at] = mixed.astype(BF16)

    if halves:
        for c, (start, size) in enumerate(CHUNKS):
            m_copy(0, c).wait_recv()
            m_copy(1, c).wait_recv()
            each_tile(start, size // 16, 16, meet)
        for j in range(2):
            half_copy(j, 0, core).start()
    elif len(late) == 2 and late[0] == 0:
        pass_on()

    def p_copy(d):
        zs = (z + d) % 4
        return send(psend.at[zs], precv.at[zs], p_ss.at[d], p_rs.at[d], pair)

    w_copy(2).wait_recv()

    def input_step(n, carry):
        rg = 1 - n // 2
        hs = n % 2
        hd[...] = dot(weights[hs, 2 * HID:3 * HID], rows[rg, 1].reshape(COLS, D), NT)

        def body(at):
            low = pl.ds(at.start + HID, at.size)
            g = gu[2 * rg + hs, at]
            u = gu[2 * rg + hs, low]
            h = hd[at]
            s = jax.nn.sigmoid(g)
            gug[at] = (h * u * s * (1.0 + g * (1.0 - s))).astype(BF16)
            gug[low] = (h * (g * s)).astype(BF16)

        each_tile(0, HID // 32, 32, body)
        def accumulate(i, carry):
            at = pl.ds(pl.multiple_of(i * WIDE, WIDE), WIDE)
            share = dot(gug[...], weights[hs, 0:2 * HID, at], TN)

            @pl.when(hs == 0)
            def _():
                part[:, at] = share

            @pl.when(hs == 1)
            def _():
                part[:, at] += share

            return carry

        lax.fori_loop(0, D // WIDE, accumulate, 0)

        @pl.when(n == 1)
        def _():
            def ready(at):
                psend[(at.start // CAP), pl.ds(at.start % CAP, 16)] = part[at].astype(BF16)

            each_tile(0, COLS // 16, 16, ready)
            p_copy(2).start()
            p_copy(1).start()

        return carry

    lax.fori_loop(0, 4, input_step, 0)
    p_copy(2).wait_send()
    p_copy(3).start()
    p_copy(1).wait_send()
    p_copy(0).start()

    def r_copy(d):
        return send(zsend.at[d], ret.at[4 - d], r_ss.at[d], r_rs.at[4 - d], at_z(d))

    for d in (2, 1, 3, 0):
        p_copy(d).wait_recv()
        zs = (z + d) % 4
        to = ret if d == 0 else zsend

        def add(at):
            mine = part[pl.ds(pl.multiple_of(zs * CAP + at.start, 16), 16)]
            to[d, at] = (mine + precv[zs, at].astype(F32)).astype(BF16)

        each_tile(0, CAP // 16, 16, add)
        if d != 0:
            r_copy(d).start()

    if halves:
        for j in range(2):
            half_copy(j, 0, core).wait_recv()
            half_copy(j, 1, core).start()
    elif len(late) == 2 and late[0] != 0:
        pass_on()
    def conclude():
        last = 2 if halves else len(late) - 1
        if halves:
            for j in range(2):
                half_copy(j, 1, 1 - core).wait_recv()

        def finish(at):
            new_ref[at] = mixed_by(last, at).astype(BF16)

        for c, (start, size) in enumerate(CHUNKS):
            if not halves:
                m_copy(last, c).wait_recv()
            each_tile(start, size // 16, 16, finish)

    if late == (0,):
        conclude()
    for d in (1, 3, 2):
        r_copy(d).wait_recv()

    def collect(i, carry):
        at = pl.ds(pl.multiple_of(i * WIDE, WIDE), WIDE)
        found = dot(spread[...], ret[:, :, at].reshape(COLS, WIDE), TN)
        out_ref[:, at] = found.astype(BF16)
        return carry

    lax.fori_loop(0, D // WIDE, collect, 0)
    if late != (0,):
        conclude()

    z_copy(2).wait_send()
    p_copy(3).wait_send()
    p_copy(0).wait_send()
    for d in (1, 2, 3):
        r_copy(d).wait_send()
    for d in range(4):
        a_copy(d).wait_send()
    w_copy(2).wait_send()
    if halves:
        for j in range(2):
            half_copy(j, 0, core).wait_send()
            half_copy(j, 1, core).wait_send()
    for c in range(len(CHUNKS)):
        if c >= len(CHUNKS) - 2:
            g_copy(c).wait_send()
        for i in range(len(late)):
            m_copy(i, c).wait_send()


def layer(late, number, *arrays):
    vmem = pl.BlockSpec(memory_space=pltpu.VMEM)
    hbm = pl.BlockSpec(memory_space=pl.ANY)
    dma = pltpu.SemaphoreType.DMA
    slots = 3 if len(late) == 2 and late[1] == 0 else len(late)
    return pl.pallas_call(
        partial(layer_kernel, late),
        out_shape=(
            jax.ShapeDtypeStruct((TOK, D), BF16),
            jax.ShapeDtypeStruct((HID, D), BF16),
        ),
        in_specs=[vmem] * 4 + [hbm] * 5,
        out_specs=(vmem, vmem),
        scratch_shapes=[
            pltpu.VMEM((4, 2, CAP, D), BF16),
            pltpu.VMEM((COLS, TOK), BF16),
            pltpu.VMEM((2, 2, 4, CAP, D), BF16),
            pltpu.VMEM((2, 3 * HID, D), BF16),
            pltpu.VMEM((4, 2 * HID, COLS), F32),
            pltpu.VMEM((HID, COLS), F32),
            pltpu.VMEM((2 * HID, COLS), BF16),
            pltpu.VMEM((HID, COLS), BF16),
            pltpu.VMEM((COLS, D), F32),
            pltpu.VMEM((2, HID, D), F32),
            pltpu.VMEM((HID, D), BF16),
            pltpu.VMEM((HID, D), BF16),
            pltpu.VMEM((4, CAP, D), BF16),
            pltpu.VMEM((4, CAP, D), BF16),
            pltpu.VMEM((4, CAP, D), BF16),
            pltpu.VMEM((4, CAP, D), BF16),
            pltpu.VMEM((slots, HID, D), BF16),
            pltpu.VMEM((slots, HID, D), BF16),
            pltpu.VMEM((2, HID, D), BF16),
            dma((4,)),
            dma((4,)),
            dma((4,)),
            dma((4,)),
            dma((3,)),
            dma((3,)),
            dma((len(CHUNKS),)),
            dma((len(CHUNKS),)),
            dma((4,)),
            dma((4,)),
            dma((4,)),
            dma((4,)),
            dma((slots, len(CHUNKS))),
            dma((slots, len(CHUNKS))),
            dma((3,)),
            dma((3,)),
        ],
        compiler_params=pltpu.CompilerParams(
            collective_id=number, has_side_effects=True, vmem_limit_bytes=56 * 2**20
        ),
        cost_estimate=pl.CostEstimate(
            flops=7 * 10**9, bytes_accessed=6 * 10**6, transcendentals=10**6
        ),
    )(*arrays)


def from_peer(state, bit):
    count = lax.axis_size("rep")
    pairs = [(source, source ^ (1 << bit)) for source in range(count)]
    return lax.ppermute(state, "rep", pairs)


def average(state, bit):
    peer = from_peer(state, bit)
    return ((state.astype(F32) + peer.astype(F32)) * 0.5).astype(BF16)


def average_with_core(state, bit):
    state = average(state, 0)
    first = lax.axis_index("rep") % 2 == 0
    top, low = state[:HALF], state[HALF:]
    mine = from_peer(jnp.where(first, top, low), bit)
    other = from_peer(mine, 0)
    peer = jnp.where(first, jnp.stack([mine, other]), jnp.stack([other, mine]))
    peer = peer.reshape(state.shape)
    return ((state.astype(F32) + peer.astype(F32)) * 0.5).astype(BF16)


def shards(
    tokens,
    cotangent,
    route_ids,
    route_weights,
    gate_weight,
    up_weight,
    down_weight,
    tracker,
    grad_prev,
    gossip_step,
):
    steps = jnp.clip(gossip_step, 0, 2)
    place = lax.broadcasted_iota(jnp.int32, (3,), 0)
    code = jnp.sum(steps * jnp.where(place == 0, 9, jnp.where(place == 1, 3, 1)), keepdims=True)
    number = lax.broadcasted_iota(jnp.int32, (2, 32), 1)
    s1, s2, s3 = number // 9, number // 3 % 3, number % 3
    early = jnp.where((s1 == s2) | (s1 == s3), 0, s1 + 1)
    early = jnp.where((early > 1) & ((s2 == 0) | (s3 == 0)), early + 2, early)
    pick = jnp.where(s2 == s3, s2, 3 + 2 * s2 + jnp.where(s3 > s2, s3 - 1, s3))
    table = jnp.where(lax.broadcasted_iota(jnp.int32, (2, 32), 0) == 0, early, pick)
    choice = jnp.sum(jnp.where(number == code, table, 0), axis=1)
    choice = lax.optimization_barrier(choice)
    early, pick = choice[0], choice[1]
    maybe = [lambda state: state] + [partial(average, bit=bit) for bit in range(3)]
    maybe += [partial(average_with_core, bit=bit) for bit in (1, 2)]
    start = lax.switch(early, maybe, tracker[0])
    out, new = lax.switch(
        pick,
        [partial(layer, late, number) for number, late in enumerate(LATE)],
        tokens[0],
        cotangent[0],
        route_ids[0].T,
        route_weights[0].T,
        gate_weight[0].T,
        up_weight[0].T,
        down_weight[0],
        start,
        grad_prev[0],
    )
    return (out[None], new[None])


def solution(mesh):
    rows = P("rep", "exp", None)
    cols = P("rep", None, "exp")
    in_specs = (rows, rows, rows, rows, cols, cols, rows, rows, rows, P())
    return jax.shard_map(
        shards, mesh=mesh, in_specs=in_specs, out_specs=(rows, rows), check_vma=False
    )
```
